32 devices in a mesh: aux: 4 (over y, core), virt: 8 (over z, x).
Axes of the slice: x: 2, y: 2, z: 4, core: 2. Of those that a mesh axis runs over, the one named last changes fastest.
Arguments:
- integrals: float32 [1024, 6, 2560], P('virt', None, 'aux'), may hold values from -1.25 to 1.25
- metric_root: float32 [2560, 2560], P(None, 'aux'), may hold values from -0.125 to 0.125
- occ_energy: float32 [256], replicated, may hold values from -1.5 to -0.3
- virt_energy: float32 [1024], replicated, may hold values from 0.2 to 3
- batch_index: int32 [6], replicated, may hold values from 0 to 255, as said below
- virt_order: int32 [1024], replicated, may hold values from 0 to 1023, each once
Outputs:
- density: float32 [1024, 6, 2560], P('virt', None, 'aux')
The draws below stay inside these ranges and needn't reach their ends.
Inputs may be any that keep to these rules, and one draw needn't show every extreme that they name: `batch_index`: 6 distinct occupied orbital numbers, among them 0 and 255. `virt_order`: each number appears once.
All inputs are finite; a program needn't handle non-finite values.
Results may differ from the reference program's by a relative error of at most 0.000057.
Values sent between devices are 32-bit elements; how exact they have to be, the bound alone decides.
A program may use at most 192 MiB of HBM per device.

```python
import jax
import jax.numpy as jnp
from jax import lax

NV = 1024
NAUX = 2560
NOCC_ALL = 256
OB = 6


def draw_batch_index(key, part):
    first_key = jax.random.fold_in(key, 11)
    second_key = jax.random.fold_in(key, 23)
    middle = (jax.random.permutation(first_key, NOCC_ALL - 2)[:OB - 2] + 1).astype(jnp.int32)
    ends = jnp.array([0, NOCC_ALL - 1], dtype=jnp.int32)
    chosen = jnp.concatenate([ends, middle], axis=0)
    return jax.random.permutation(second_key, chosen).astype(jnp.int32)


def steps_of(key, extent, cuts, least, high):
    def one(axis_at, parts):
        heights = jax.random.uniform(jax.random.fold_in(jax.random.fold_in(key, 6), axis_at), (parts,), jnp.float32, least / len(cuts), high / len(cuts))
        return jnp.repeat(jnp.exp(heights), extent[axis_at] // parts).reshape((-1,) + (1,) * (len(extent) - axis_at - 1))

    factor_of = one(*cuts[0])
    for cut in cuts[1:]:
        factor_of = factor_of * one(*cut)
    return factor_of


def scatter_about(rng, dims, width, reach, shards=(), kind=jnp.bfloat16):
    result = jax.random.normal(rng, dims, jnp.float32) * width
    if len(shards) > 0:
        result = steps_of(rng, dims, shards, -0.22, 0.18) * result
    return jnp.clip(result, min=-reach, max=reach).astype(kind)


def setup_inputs(seed: int = 0) -> dict:
    seeds = jax.random.split(jax.random.key(seed), 7)
    integrals = scatter_about(seeds[0], (NV, OB, NAUX), 0.09, 1.25, ((0, 8), (2, 4)), jnp.float32)
    metric_root = scatter_about(seeds[1], (NAUX, NAUX), NAUX ** -0.5, 0.125, ((1, 4),), jnp.float32)
    occ_energy = jnp.clip(jax.random.uniform(seeds[2], (NOCC_ALL,), jnp.float32, -1.5, -0.3), -1.5, -0.3)
    virt_energy = jnp.clip(jax.random.uniform(seeds[3], (NV,), jnp.float32, 0.2, 3.0), 0.2, 3.0)
    batch_index = draw_batch_index(jax.random.fold_in(seeds[6], 71), 0)
    virt_order = jax.random.permutation(seeds[5], NV).astype(jnp.int32)
    return {"integrals": integrals, "metric_root": metric_root, "occ_energy": occ_energy, "virt_energy": virt_energy, "batch_index": batch_index, "virt_order": virt_order}


precise = lax.Precision.HIGHEST
block_size = 64


def pair_density(left_rows, right_rows, row_levels, col_levels, occ_levels):
    row_count = row_levels.shape[0]
    col_count = col_levels.shape[0]
    occ_count = occ_levels.shape[0]
    pair_ints = lax.dot_general(left_rows, right_rows, (((1,), (1,)), ((), ())), precision=precise, preferred_element_type=jnp.float32)
    pair_ints = pair_ints.reshape(row_count, occ_count, col_count, occ_count)
    swapped = pair_ints.transpose(0, 3, 2, 1)
    denominator = occ_levels[None, :, None, None] + occ_levels[None, None, None, :] - row_levels[:, None, None, None] - col_levels[None, None, :, None]
    weighted = ((2.0 * pair_ints - swapped) / denominator).reshape(row_count * occ_count, col_count * occ_count)
    return jnp.dot(weighted, right_rows, precision=precise, preferred_element_type=jnp.float32)


def reference(integrals, metric_root, occ_energy, virt_energy, batch_index, virt_order):
    virt_total, batch_count, aux_total = integrals.shape
    occ_levels = occ_energy[batch_index]
    virt_levels = virt_energy[virt_order]
    flattened = integrals.reshape(virt_total * batch_count, aux_total)
    fitted = lax.dot_general(flattened, metric_root, (((1,), (1,)), ((), ())), precision=precise, preferred_element_type=jnp.float32)

    def block_density(start_row):
        left_rows = lax.dynamic_slice_in_dim(fitted, start_row * batch_count, block_size * batch_count, 0)
        row_levels = lax.dynamic_slice_in_dim(virt_levels, start_row, block_size, 0)
        return pair_density(left_rows, fitted, row_levels, virt_levels, occ_levels)

    block_starts = (jnp.arange(virt_total // block_size) * block_size).astype(jnp.int32)
    blocks = lax.map(block_density, block_starts)
    return blocks.reshape(virt_total, batch_count, aux_total)
```

```python
import jax
import jax.numpy as jnp
from jax import lax
from jax.sharding import PartitionSpec as P

precise = lax.Precision.HIGH


def select_levels(levels_table, picked):
    places = jnp.arange(levels_table.shape[0], dtype=jnp.int32)
    return jnp.sum(
        jnp.where(picked[:, None] == places[None, :], levels_table[None, :], 0.0), axis=1
    )


def shards(integrals, metric_root, occ_energy, virt_energy, batch_index, virt_order):
    virt_local, batch_count, aux_local = integrals.shape
    aux_total = metric_root.shape[0]
    aux_count = lax.axis_size("aux")
    virt_count = lax.axis_size("virt")
    aux_place = lax.axis_index("aux")
    virt_place = lax.axis_index("virt")
    share = virt_local // aux_count
    occ_levels = select_levels(occ_energy, batch_index)
    virt_levels = select_levels(virt_energy, virt_order)
    row_levels = lax.dynamic_slice_in_dim(virt_levels, virt_place * virt_local, virt_local, 0)
    col_levels = lax.dynamic_slice_in_dim(
        virt_levels.reshape(virt_count, aux_count, share), aux_place, 1, 1
    ).reshape(virt_count * share)

    by_occ = integrals.transpose(1, 0, 2).reshape(batch_count * virt_local, aux_local)
    partial_term = lax.dot_general(
        by_occ,
        metric_root,
        (((1,), (1,)), ((), ())),
        precision=precise,
        preferred_element_type=jnp.float32,
    ).reshape(batch_count, virt_local, aux_total)
    own = lax.psum_scatter(partial_term, "aux", scatter_dimension=1, tiled=True)
    rows = lax.all_gather(own, "aux", axis=1, tiled=True)
    cols = lax.all_gather(own, "virt", axis=1, tiled=True)
    col_count = virt_count * share
    rows2 = rows.reshape(batch_count * virt_local, aux_total)
    cols2 = cols.reshape(batch_count * col_count, aux_total)
    pair = lax.dot_general(
        rows2,
        cols2,
        (((1,), (1,)), ((), ())),
        precision=precise,
        preferred_element_type=jnp.float32,
    ).reshape(batch_count, virt_local, batch_count, col_count)
    swapped = pair.transpose(2, 1, 0, 3)
    denominator = (
        occ_levels[:, None, None, None]
        + occ_levels[None, None, :, None]
        - row_levels[None, :, None, None]
        - col_levels[None, None, None, :]
    )
    weighted = ((2.0 * pair - swapped) / denominator).reshape(
        batch_count * virt_local, batch_count * col_count
    )
    density = jnp.dot(weighted, cols2, precision=precise, preferred_element_type=jnp.float32)
    result = lax.psum_scatter(density, "aux", scatter_dimension=1, tiled=True)
    return result.reshape(batch_count, virt_local, aux_local).transpose(1, 0, 2)


def solution(mesh):
    return jax.shard_map(
        shards,
        mesh=mesh,
        in_specs=(P("virt", None, "aux"), P(None, "aux"), P(), P(), P(), P()),
        out_specs=P("virt", None, "aux"),
        check_vma=False,
    )
```

```python
import functools

import jax
import jax.numpy as jnp
from jax import lax
from jax.experimental import pallas as pl
from jax.experimental.pallas import tpu as pltpu
from jax.sharding import PartitionSpec as P

precise = lax.Precision.HIGH


def select_levels(levels_table, picked):
    places = jnp.arange(levels_table.shape[0], dtype=jnp.int32)
    return jnp.sum(
        jnp.where(picked[:, None] == places[None, :], levels_table[None, :], 0.0), axis=1
    )


def ring_member(place, count):
    return jnp.where(place < count // 2, 2 * place, 2 * (count - 1 - place) + 1)


def ring_place(member, count):
    return jnp.where(lax.rem(member, 2) == 0, member // 2, count - 1 - member // 2)


def gather_kernel(
    aux_count, virt_count, partial, rows, cols, pairsum, arrived, own,
    sib_send, sib_recv, far_send, far_recv, row_send, row_recv, pass_send, pass_recv,
    ring_send, ring_recv, local_sem,
):
    occs, far_count, _, share, _ = partial.shape
    aux_place = lax.axis_index("aux")
    virt_place = lax.axis_index("virt")
    core = lax.rem(aux_place, 2)
    far_place = aux_place // 2
    sibling = {"aux": far_place * 2 + 1 - core}
    fars = [lax.rem(far_place + hop, far_count) for hop in range(1, far_count)]
    place = ring_place(virt_place, virt_count)
    ahead = {"virt": ring_member(lax.rem(place + 1, virt_count), virt_count)}
    behind = {"virt": ring_member(lax.rem(place + virt_count - 1, virt_count), virt_count)}

    def remote(source, target, send, recv, device):
        return pltpu.make_async_remote_copy(
            src_ref=source, dst_ref=target, send_sem=send, recv_sem=recv,
            device_id=device, device_id_type=pl.DeviceIdType.MESH,
        )

    barrier = pltpu.get_barrier_semaphore()
    partners = [sibling, ahead, behind] + [{"aux": far * 2 + core} for far in fars]
    for partner in partners:
        pl.semaphore_signal(barrier, inc=1, device_id=partner, device_id_type=pl.DeviceIdType.MESH)
    pl.semaphore_wait(barrier, len(partners))

    forward = (occs + 1) // 2
    order = []
    for occ in range(forward):
        order.append(occ)
        if forward + occ < occs:
            order.append(forward + occ)

    sib_copies = {}
    for occ in order:
        copy = remote(
            partial.at[occ, :, 1 - core], pairsum.at[occ], sib_send.at[occ], sib_recv.at[occ], sibling
        )
        copy.start()
        sib_copies[occ] = copy
    far_copies = {}
    for occ in order:
        sib_copies[occ].wait_recv()
        pairsum[occ] = pairsum[occ] + partial[occ, :, core]
        for hop, far in enumerate(fars):
            copy = remote(
                pairsum.at[occ, far], arrived.at[occ, hop], far_send.at[occ, hop],
                far_recv.at[occ, hop], {"aux": far * 2 + core},
            )
            copy.start()
            far_copies[occ, hop] = copy

    def ring_copy(occ, step):
        cw = occ < forward
        origin = lax.rem(place + (virt_count - step if cw else step), virt_count)
        slot = cols.at[occ, pl.ds(pl.multiple_of(ring_member(origin, virt_count) * share, share), share)]
        source = own.at[occ] if step == 0 else slot
        return remote(
            source, slot, ring_send.at[occ, step], ring_recv.at[occ, step], ahead if cw else behind
        )

    def row_slot(occ, member):
        return rows.at[occ, pl.ds(pl.multiple_of(member * share, share), share)]

    ring = {}
    row_copies = {}
    pass_copies = {}
    local = []
    for occ in order:
        for hop in range(len(fars)):
            far_copies[occ, hop].wait_recv()
        total = pairsum[occ, far_place]
        for hop in range(len(fars)):
            total = total + arrived[occ, hop]
        own[occ] = total
        ring[occ, 0] = ring_copy(occ, 0)
        ring[occ, 0].start()
        for hop, far in enumerate(fars):
            copy = remote(
                own.at[occ], row_slot(occ, aux_place), row_send.at[occ, hop],
                row_recv.at[occ, hop], {"aux": far * 2 + core},
            )
            copy.start()
            row_copies[occ, hop] = copy
        copy = remote(
            own.at[occ], row_slot(occ, aux_place), pass_send.at[occ, 0], pass_recv.at[occ, 0], sibling
        )
        copy.start()
        pass_copies[occ, 0] = copy
        copy = pltpu.make_async_copy(own.at[occ], row_slot(occ, aux_place), local_sem.at[occ, 0])
        copy.start()
        local.append(copy)
        mine = cols.at[occ, pl.ds(pl.multiple_of(virt_place * share, share), share)]
        copy = pltpu.make_async_copy(own.at[occ], mine, local_sem.at[occ, 1])
        copy.start()
        local.append(copy)

    for step in range(1, virt_count - 1):
        for occ in order:
            ring[occ, step - 1].wait_recv()
            ring[occ, step] = ring_copy(occ, step)
            ring[occ, step].start()
        if step == 3:
            for occ in order:
                for hop in range(len(fars)):
                    row_copies[occ, hop].wait_recv()
                    sender = lax.rem(far_place + far_count - 1 - hop, far_count) * 2 + core
                    copy = remote(
                        row_slot(occ, sender), row_slot(occ, sender), pass_send.at[occ, hop + 1],
                        pass_recv.at[occ, hop + 1], sibling,
                    )
                    copy.start()
                    pass_copies[occ, hop + 1] = copy
    for occ in order:
        ring[occ, virt_count - 2].wait_recv()
    for copy in pass_copies.values():
        copy.wait_recv()
    for copy in local:
        copy.wait()
    for group in (sib_copies, far_copies, ring, row_copies, pass_copies):
        for copy in group.values():
            copy.wait_send()


def gather_fitted(partial_term, aux_count, virt_count):
    occs, virt_local, aux_total = partial_term.shape
    share = virt_local // aux_count
    far_count = aux_count // 2
    dma = pltpu.SemaphoreType.DMA
    return pl.pallas_call(
        functools.partial(gather_kernel, aux_count, virt_count),
        out_shape=(
            jax.ShapeDtypeStruct((occs, virt_local, aux_total), jnp.float32),
            jax.ShapeDtypeStruct((occs, virt_count * share, aux_total), jnp.float32),
        ),
        in_specs=[pl.BlockSpec(memory_space=pltpu.VMEM)],
        out_specs=(pl.BlockSpec(memory_space=pl.ANY), pl.BlockSpec(memory_space=pl.ANY)),
        scratch_shapes=[
            pltpu.VMEM((occs, far_count, share, aux_total), jnp.float32),
            pltpu.VMEM((occs, far_count - 1, share, aux_total), jnp.float32),
            pltpu.VMEM((occs, share, aux_total), jnp.float32),
            dma((occs,)), dma((occs,)),
            dma((occs, far_count - 1)), dma((occs, far_count - 1)),
            dma((occs, far_count - 1)), dma((occs, far_count - 1)),
            dma((occs, far_count)), dma((occs, far_count)),
            dma((occs, virt_count - 1)), dma((occs, virt_count - 1)),
            dma((occs, 2)),
        ],
        compiler_params=pltpu.CompilerParams(
            collective_id=0, has_side_effects=True, vmem_limit_bytes=40 * 1024 * 1024
        ),
        cost_estimate=pl.CostEstimate(flops=0, bytes_accessed=4 * 6 * occs * virt_local * aux_total, transcendentals=0),
    )(partial_term.reshape(occs, far_count, 2, share, aux_total))


def shards(integrals, metric_root, occ_energy, virt_energy, batch_index, virt_order):
    virt_local, batch_count, aux_local = integrals.shape
    aux_total = metric_root.shape[0]
    aux_count = lax.axis_size("aux")
    virt_count = lax.axis_size("virt")
    aux_place = lax.axis_index("aux")
    virt_place = lax.axis_index("virt")
    share = virt_local // aux_count
    occ_levels = select_levels(occ_energy, batch_index)
    virt_levels = select_levels(virt_energy, virt_order)
    row_levels = lax.dynamic_slice_in_dim(virt_levels, virt_place * virt_local, virt_local, 0)
    col_levels = lax.dynamic_slice_in_dim(
        virt_levels.reshape(virt_count, aux_count, share), aux_place, 1, 1
    ).reshape(virt_count * share)

    by_occ = integrals.transpose(1, 0, 2).reshape(batch_count * virt_local, aux_local)
    partial_term = lax.dot_general(
        by_occ,
        metric_root,
        (((1,), (1,)), ((), ())),
        precision=precise,
        preferred_element_type=jnp.float32,
    ).reshape(batch_count, virt_local, aux_total)
    rows, cols = gather_fitted(partial_term, aux_count, virt_count)
    col_count = virt_count * share
    rows2 = rows.reshape(batch_count * virt_local, aux_total)
    cols2 = cols.reshape(batch_count * col_count, aux_total)
    pair = lax.dot_general(
        rows2,
        cols2,
        (((1,), (1,)), ((), ())),
        precision=precise,
        preferred_element_type=jnp.float32,
    ).reshape(batch_count, virt_local, batch_count, col_count)
    swapped = pair.transpose(2, 1, 0, 3)
    denominator = (
        occ_levels[:, None, None, None]
        + occ_levels[None, None, :, None]
        - row_levels[None, :, None, None]
        - col_levels[None, None, None, :]
    )
    weighted = ((2.0 * pair - swapped) / denominator).reshape(
        batch_count * virt_local, batch_count * col_count
    )
    density = jnp.dot(weighted, cols2, precision=precise, preferred_element_type=jnp.float32)
    result = lax.psum_scatter(density, "aux", scatter_dimension=1, tiled=True)
    return result.reshape(batch_count, virt_local, aux_local).transpose(1, 0, 2)


def solution(mesh):
    return jax.shard_map(
        shards,
        mesh=mesh,
        in_specs=(P("virt", None, "aux"), P(None, "aux"), P(), P(), P(), P()),
        out_specs=P("virt", None, "aux"),
        check_vma=False,
    )
```

```python
import functools

import jax
import jax.numpy as jnp
from jax import lax
from jax.experimental import pallas as pl
from jax.experimental.pallas import tpu as pltpu
from jax.sharding import PartitionSpec as P

precise = lax.Precision.HIGH


def select_levels(levels_table, picked):
    places = jnp.arange(levels_table.shape[0], dtype=jnp.int32)
    return jnp.sum(
        jnp.where(picked[:, None] == places[None, :], levels_table[None, :], 0.0), axis=1
    )


def ring_member(place, count):
    return jnp.where(place < count // 2, 2 * place, 2 * (count - 1 - place) + 1)


def ring_place(member, count):
    return jnp.where(lax.rem(member, 2) == 0, member // 2, count - 1 - member // 2)


def gather_kernel(
    aux_count, virt_count, partial, rows, cols, pairsum, arrived, own,
    sib_send, sib_recv, far_send, far_recv, row_send, row_recv, pass_send, pass_recv,
    ring_send, ring_recv, local_sem,
):
    occs, far_count, _, share, _ = partial.shape
    aux_place = lax.axis_index("aux")
    virt_place = lax.axis_index("virt")
    core = lax.rem(aux_place, 2)
    far_place = aux_place // 2
    sibling = {"aux": far_place * 2 + 1 - core}
    fars = [lax.rem(far_place + hop, far_count) for hop in range(1, far_count)]
    place = ring_place(virt_place, virt_count)
    ahead = {"virt": ring_member(lax.rem(place + 1, virt_count), virt_count)}
    behind = {"virt": ring_member(lax.rem(place + virt_count - 1, virt_count), virt_count)}

    def remote(source, target, send, recv, device):
        return pltpu.make_async_remote_copy(
            src_ref=source, dst_ref=target, send_sem=send, recv_sem=recv,
            device_id=device, device_id_type=pl.DeviceIdType.MESH,
        )

    barrier = pltpu.get_barrier_semaphore()
    partners = [sibling, ahead, behind] + [{"aux": far * 2 + core} for far in fars]
    for partner in partners:
        pl.semaphore_signal(barrier, inc=1, device_id=partner, device_id_type=pl.DeviceIdType.MESH)
    pl.semaphore_wait(barrier, len(partners))

    forward = (occs + 1) // 2
    order = []
    for occ in range(forward):
        order.append(occ)
        if forward + occ < occs:
            order.append(forward + occ)

    sib_copies = {}
    for occ in order:
        copy = remote(
            partial.at[occ, :, 1 - core], pairsum.at[occ], sib_send.at[occ], sib_recv.at[occ], sibling
        )
        copy.start()
        sib_copies[occ] = copy
    far_copies = {}
    for occ in order:
        sib_copies[occ].wait_recv()
        pairsum[occ] = pairsum[occ] + partial[occ, :, core]
        for hop, far in enumerate(fars):
            copy = remote(
                pairsum.at[occ, far], arrived.at[occ, hop], far_send.at[occ, hop],
                far_recv.at[occ, hop], {"aux": far * 2 + core},
            )
            copy.start()
            far_copies[occ, hop] = copy

    def ring_copy(occ, step):
        cw = occ < forward
        origin = lax.rem(place + (virt_count - step if cw else step), virt_count)
        slot = cols.at[occ, pl.ds(pl.multiple_of(ring_member(origin, virt_count) * share, share), share)]
        source = own.at[occ] if step == 0 else slot
        return remote(
            source, slot, ring_send.at[occ, step], ring_recv.at[occ, step], ahead if cw else behind
        )

    def row_slot(occ, member):
        return rows.at[occ, pl.ds(pl.multiple_of(member * share, share), share)]

    ring = {}
    row_copies = {}
    pass_copies = {}
    local = []
    for occ in order:
        for hop in range(len(fars)):
            far_copies[occ, hop].wait_recv()
        total = pairsum[occ, far_place]
        for hop in range(len(fars)):
            total = total + arrived[occ, hop]
        own[occ] = total
        ring[occ, 0] = ring_copy(occ, 0)
        ring[occ, 0].start()
        for hop, far in enumerate(fars):
            copy = remote(
                own.at[occ], row_slot(occ, aux_place), row_send.at[occ, hop],
                row_recv.at[occ, hop], {"aux": far * 2 + core},
            )
            copy.start()
            row_copies[occ, hop] = copy
        copy = remote(
            own.at[occ], row_slot(occ, aux_place), pass_send.at[occ, 0], pass_recv.at[occ, 0], sibling
        )
        copy.start()
        pass_copies[occ, 0] = copy
        copy = pltpu.make_async_copy(own.at[occ], row_slot(occ, aux_place), local_sem.at[occ, 0])
        copy.start()
        local.append(copy)
        mine = cols.at[occ, pl.ds(pl.multiple_of(virt_place * share, share), share)]
        copy = pltpu.make_async_copy(own.at[occ], mine, local_sem.at[occ, 1])
        copy.start()
        local.append(copy)

    for step in range(1, virt_count - 1):
        for occ in order:
            ring[occ, step - 1].wait_recv()
            ring[occ, step] = ring_copy(occ, step)
            ring[occ, step].start()
        if step == 3:
            for occ in order:
                for hop in range(len(fars)):
                    row_copies[occ, hop].wait_recv()
                    sender = lax.rem(far_place + far_count - 1 - hop, far_count) * 2 + core
                    copy = remote(
                        row_slot(occ, sender), row_slot(occ, sender), pass_send.at[occ, hop + 1],
                        pass_recv.at[occ, hop + 1], sibling,
                    )
                    copy.start()
                    pass_copies[occ, hop + 1] = copy
    for occ in order:
        ring[occ, virt_count - 2].wait_recv()
    for copy in pass_copies.values():
        copy.wait_recv()
    for copy in local:
        copy.wait()
    for group in (sib_copies, far_copies, ring, row_copies, pass_copies):
        for copy in group.values():
            copy.wait_send()


def gather_fitted(partial_term, aux_count, virt_count):
    occs, virt_local, aux_total = partial_term.shape
    share = virt_local // aux_count
    far_count = aux_count // 2
    dma = pltpu.SemaphoreType.DMA
    return pl.pallas_call(
        functools.partial(gather_kernel, aux_count, virt_count),
        out_shape=(
            jax.ShapeDtypeStruct((occs, virt_local, aux_total), jnp.float32),
            jax.ShapeDtypeStruct((occs, virt_count * share, aux_total), jnp.float32),
        ),
        in_specs=[pl.BlockSpec(memory_space=pltpu.VMEM)],
        out_specs=(pl.BlockSpec(memory_space=pl.ANY), pl.BlockSpec(memory_space=pl.ANY)),
        scratch_shapes=[
            pltpu.VMEM((occs, far_count, share, aux_total), jnp.float32),
            pltpu.VMEM((occs, far_count - 1, share, aux_total), jnp.float32),
            pltpu.VMEM((occs, share, aux_total), jnp.float32),
            dma((occs,)), dma((occs,)),
            dma((occs, far_count - 1)), dma((occs, far_count - 1)),
            dma((occs, far_count - 1)), dma((occs, far_count - 1)),
            dma((occs, far_count)), dma((occs, far_count)),
            dma((occs, virt_count - 1)), dma((occs, virt_count - 1)),
            dma((occs, 2)),
        ],
        compiler_params=pltpu.CompilerParams(
            collective_id=0, has_side_effects=True, vmem_limit_bytes=40 * 1024 * 1024
        ),
        cost_estimate=pl.CostEstimate(flops=0, bytes_accessed=4 * 6 * occs * virt_local * aux_total, transcendentals=0),
    )(partial_term.reshape(occs, far_count, 2, share, aux_total))


def split_parts(values):
    high = values.astype(jnp.bfloat16)
    return high, (values - high.astype(jnp.float32)).astype(jnp.bfloat16)


def density_kernel(
    aux_count, pair, occ_levels, row_levels, col_levels, cols, out,
    w_high, w_low, stage, c_high, c_low, partial, from_sib, from_far,
    stage_sem, sib_send, sib_recv, far_send, far_recv,
):
    occs, virt_local, width = out.shape
    rows = occs * virt_local
    half = rows // 2
    half_occs = occs // 2
    col_count = col_levels.shape[1]
    far_count = aux_count // 2
    aux_place = lax.axis_index("aux")
    core = lax.rem(aux_place, 2)
    far_place = aux_place // 2
    sibling = {"aux": far_place * 2 + 1 - core}

    def fetch(unit, slot):
        target = lax.rem(far_place + 1 + unit // 2, far_count)
        owner = target * 2 + jnp.where(lax.rem(unit, 2) == 0, 1 - core, core)
        return pltpu.make_async_copy(
            cols.at[:, pl.ds(pl.multiple_of(owner * width, 128), width)],
            stage.at[slot], stage_sem.at[slot],
        )

    def sib_copy(hop, part):
        return pltpu.make_async_remote_copy(
            src_ref=partial.at[2 * hop, part], dst_ref=from_sib.at[hop, part],
            send_sem=sib_send.at[hop, part], recv_sem=sib_recv.at[hop, part],
            device_id=sibling, device_id_type=pl.DeviceIdType.MESH,
        )

    def far_copy(hop, part):
        target = lax.rem(far_place + 1 + hop, far_count)
        return pltpu.make_async_remote_copy(
            src_ref=partial.at[2 * hop + 1, part], dst_ref=from_far.at[hop, part],
            send_sem=far_send.at[hop, part], recv_sem=far_recv.at[hop, part],
            device_id={"aux": target * 2 + core}, device_id_type=pl.DeviceIdType.MESH,
        )

    barrier = pltpu.get_barrier_semaphore()
    partners = [sibling] + [
        {"aux": lax.rem(far_place + hop, far_count) * 2 + core} for hop in range(1, far_count)
    ]
    for partner in partners:
        pl.semaphore_signal(barrier, inc=1, device_id=partner, device_id_type=pl.DeviceIdType.MESH)
    fetch(0, 0).start()

    for i in range(occs):
        for j in range(occs):
            direct = pair[pl.ds(i * virt_local, virt_local), pl.ds(j * col_count, col_count)]
            crossed = pair[pl.ds(j * virt_local, virt_local), pl.ds(i * col_count, col_count)]
            denominator = occ_levels[i] + occ_levels[j] - row_levels[...] - col_levels[...]
            high, low = split_parts((2.0 * direct - crossed) / denominator)
            w_high[pl.ds(i * virt_local, virt_local), pl.ds(j * col_count, col_count)] = high
            w_low[pl.ds(i * virt_local, virt_local), pl.ds(j * col_count, col_count)] = low
    pl.semaphore_wait(barrier, len(partners))

    depth = w_high.shape[1]
    units = 2 * far_count
    pieces = occs
    piece = depth // pieces
    for unit in range(units):
        slot = unit % 2
        hop = unit // 2
        if unit + 1 < units:
            fetch(unit + 1, 1 - slot).start()
        fetch(unit, slot).wait()

        @pl.loop(0, pieces)
        def _(step):
            where = pl.ds(pl.multiple_of(step * piece, piece), piece)
            high, low = split_parts(stage[slot, where, :])
            c_high[where, :] = high
            c_low[where, :] = low

        @pl.loop(0, 2)
        def _(part):
            where = pl.ds(pl.multiple_of(part * half, half), half)
            left_high = w_high[where, :]
            right_high = c_high[...]
            total = jnp.dot(left_high, c_low[...], preferred_element_type=jnp.float32)
            total += jnp.dot(w_low[where, :], right_high, preferred_element_type=jnp.float32)
            total += jnp.dot(left_high, right_high, preferred_element_type=jnp.float32)
            if unit % 2 == 0:
                partial[unit, part] = total
                sib_copy(hop, part).start()
            elif hop < far_count - 1:
                sib_copy(hop, part).wait_recv()
                partial[unit, part] = total + from_sib[hop, part]
                far_copy(hop, part).start()
            else:
                sib_copy(hop, part).wait_recv()
                partial[unit, part] = total + from_sib[hop, part]

    for part in range(2):
        total = partial[units - 1, part]
        for hop in range(far_count - 1):
            far_copy(hop, part).wait_recv()
            total = total + from_far[hop, part]
        out[pl.ds(part * half_occs, half_occs)] = total.reshape(half_occs, virt_local, width)
    for part in range(2):
        for hop in range(far_count):
            sib_copy(hop, part).wait_send()
        for hop in range(far_count - 1):
            far_copy(hop, part).wait_send()


def scattered_density(pair, occ_levels, row_levels, col_levels, cols, aux_count):
    occs = occ_levels.shape[0]
    virt_local = row_levels.shape[0]
    rows, depth = pair.shape
    width = cols.shape[1] // aux_count
    far_count = aux_count // 2
    dma = pltpu.SemaphoreType.DMA
    vmem = pl.BlockSpec(memory_space=pltpu.VMEM)
    return pl.pallas_call(
        functools.partial(density_kernel, aux_count),
        out_shape=jax.ShapeDtypeStruct((occs, virt_local, width), jnp.float32),
        in_specs=[
            vmem, pl.BlockSpec(memory_space=pltpu.SMEM), vmem, vmem,
            pl.BlockSpec(memory_space=pl.ANY),
        ],
        out_specs=vmem,
        scratch_shapes=[
            pltpu.VMEM((rows, depth), jnp.bfloat16),
            pltpu.VMEM((rows, depth), jnp.bfloat16),
            pltpu.VMEM((2, depth, width), jnp.float32),
            pltpu.VMEM((depth, width), jnp.bfloat16),
            pltpu.VMEM((depth, width), jnp.bfloat16),
            pltpu.VMEM((2 * far_count, 2, rows // 2, width), jnp.float32),
            pltpu.VMEM((far_count, 2, rows // 2, width), jnp.float32),
            pltpu.VMEM((far_count - 1, 2, rows // 2, width), jnp.float32),
            dma((2,)),
            dma((far_count, 2)), dma((far_count, 2)),
            dma((far_count - 1, 2)), dma((far_count - 1, 2)),
        ],
        compiler_params=pltpu.CompilerParams(
            collective_id=1, has_side_effects=True, vmem_limit_bytes=50 * 1024 * 1024
        ),
        cost_estimate=pl.CostEstimate(
            flops=6 * rows * depth * cols.shape[1], bytes_accessed=4 * depth * cols.shape[1],
            transcendentals=0,
        ),
    )(pair, occ_levels, row_levels[:, None], col_levels[None, :], cols)


def shards(integrals, metric_root, occ_energy, virt_energy, batch_index, virt_order):
    virt_local, batch_count, aux_local = integrals.shape
    aux_total = metric_root.shape[0]
    aux_count = lax.axis_size("aux")
    virt_count = lax.axis_size("virt")
    aux_place = lax.axis_index("aux")
    virt_place = lax.axis_index("virt")
    share = virt_local // aux_count
    occ_levels = select_levels(occ_energy, batch_index)
    virt_levels = select_levels(virt_energy, virt_order)
    row_levels = lax.dynamic_slice_in_dim(virt_levels, virt_place * virt_local, virt_local, 0)
    col_levels = lax.dynamic_slice_in_dim(
        virt_levels.reshape(virt_count, aux_count, share), aux_place, 1, 1
    ).reshape(virt_count * share)

    by_occ = integrals.transpose(1, 0, 2).reshape(batch_count * virt_local, aux_local)
    partial_term = lax.dot_general(
        by_occ,
        metric_root,
        (((1,), (1,)), ((), ())),
        precision=precise,
        preferred_element_type=jnp.float32,
    ).reshape(batch_count, virt_local, aux_total)
    rows, cols = gather_fitted(partial_term, aux_count, virt_count)
    col_count = virt_count * share
    rows2 = rows.reshape(batch_count * virt_local, aux_total)
    cols2 = cols.reshape(batch_count * col_count, aux_total)
    pair = lax.dot_general(
        rows2,
        cols2,
        (((1,), (1,)), ((), ())),
        precision=precise,
        preferred_element_type=jnp.float32,
    )
    if aux_local % 128 == 0 and batch_count % 2 == 0:
        result = scattered_density(pair, occ_levels, row_levels, col_levels, cols2, aux_count)
        return result.transpose(1, 0, 2)
    pair = pair.reshape(batch_count, virt_local, batch_count, col_count)
    swapped = pair.transpose(2, 1, 0, 3)
    denominator = (
        occ_levels[:, None, None, None]
        + occ_levels[None, None, :, None]
        - row_levels[None, :, None, None]
        - col_levels[None, None, None, :]
    )
    weighted = ((2.0 * pair - swapped) / denominator).reshape(
        batch_count * virt_local, batch_count * col_count
    )
    density = jnp.dot(weighted, cols2, precision=precise, preferred_element_type=jnp.float32)
    result = lax.psum_scatter(density, "aux", scatter_dimension=1, tiled=True)
    return result.reshape(batch_count, virt_local, aux_local).transpose(1, 0, 2)


def solution(mesh):
    return jax.shard_map(
        shards,
        mesh=mesh,
        in_specs=(P("virt", None, "aux"), P(None, "aux"), P(), P(), P(), P()),
        out_specs=P("virt", None, "aux"),
        check_vma=False,
    )
```

```python
import functools

import jax
import jax.numpy as jnp
from jax import lax
from jax.experimental import pallas as pl
from jax.experimental.pallas import tpu as pltpu
from jax.sharding import PartitionSpec as P

precise = lax.Precision.HIGH


def select_levels(levels_table, picked):
    places = jnp.arange(levels_table.shape[0], dtype=jnp.int32)
    return jnp.sum(
        jnp.where(picked[:, None] == places[None, :], levels_table[None, :], 0.0), axis=1
    )


def ring_member(place, count):
    return jnp.where(place < count // 2, 2 * place, 2 * (count - 1 - place) + 1)


def ring_place(member, count):
    return jnp.where(lax.rem(member, 2) == 0, member // 2, count - 1 - member // 2)


def gather_kernel(
    aux_count, virt_count, partial, rows, cols, pairsum, arrived, own,
    sib_send, sib_recv, far_send, far_recv, row_send, row_recv, pass_send, pass_recv,
    ring_send, ring_recv, local_sem,
):
    occs, far_count, _, share, _ = partial.shape
    aux_place = lax.axis_index("aux")
    virt_place = lax.axis_index("virt")
    core = lax.rem(aux_place, 2)
    far_place = aux_place // 2
    sibling = {"aux": far_place * 2 + 1 - core}
    fars = [lax.rem(far_place + hop, far_count) for hop in range(1, far_count)]
    place = ring_place(virt_place, virt_count)
    ahead = {"virt": ring_member(lax.rem(place + 1, virt_count), virt_count)}
    behind = {"virt": ring_member(lax.rem(place + virt_count - 1, virt_count), virt_count)}

    def remote(source, target, send, recv, device):
        return pltpu.make_async_remote_copy(
            src_ref=source, dst_ref=target, send_sem=send, recv_sem=recv,
            device_id=device, device_id_type=pl.DeviceIdType.MESH,
        )

    barrier = pltpu.get_barrier_semaphore()
    partners = [sibling, ahead, behind] + [{"aux": far * 2 + core} for far in fars]
    for partner in partners:
        pl.semaphore_signal(barrier, inc=1, device_id=partner, device_id_type=pl.DeviceIdType.MESH)
    pl.semaphore_wait(barrier, len(partners))

    forward = (occs + 1) // 2
    order = []
    for occ in range(forward):
        order.append(occ)
        if forward + occ < occs:
            order.append(forward + occ)

    sib_copies = {}
    for occ in order:
        copy = remote(
            partial.at[occ, :, 1 - core], pairsum.at[occ], sib_send.at[occ], sib_recv.at[occ], sibling
        )
        copy.start()
        sib_copies[occ] = copy
    far_copies = {}
    for occ in order:
        sib_copies[occ].wait_recv()
        pairsum[occ] = pairsum[occ] + partial[occ, :, core]
        for hop, far in enumerate(fars):
            copy = remote(
                pairsum.at[occ, far], arrived.at[occ, hop], far_send.at[occ, hop],
                far_recv.at[occ, hop], {"aux": far * 2 + core},
            )
            copy.start()
            far_copies[occ, hop] = copy

    def ring_copy(occ, step):
        cw = occ < forward
        origin = lax.rem(place + (virt_count - step if cw else step), virt_count)
        slot = cols.at[occ, pl.ds(pl.multiple_of(ring_member(origin, virt_count) * share, share), share)]
        source = own.at[occ] if step == 0 else slot
        return remote(
            source, slot, ring_send.at[occ, step], ring_recv.at[occ, step], ahead if cw else behind
        )

    def row_slot(occ, member):
        return rows.at[occ, pl.ds(pl.multiple_of(member * share, share), share)]

    ring = {}
    row_copies = {}
    pass_copies = {}
    local = []
    def finish_sum(occ):
        for hop in range(len(fars)):
            far_copies[occ, hop].wait_recv()
        total = pairsum[occ, far_place]
        for hop in range(len(fars)):
            total = total + arrived[occ, hop]
        own[occ] = total
        ring[occ, 0] = ring_copy(occ, 0)
        ring[occ, 0].start()
        copy = remote(
            own.at[occ], row_slot(occ, aux_place), pass_send.at[occ, 0], pass_recv.at[occ, 0], sibling
        )
        copy.start()
        pass_copies[occ, 0] = copy
        copy = pltpu.make_async_copy(own.at[occ], row_slot(occ, aux_place), local_sem.at[occ, 0])
        copy.start()
        local.append(copy)
        mine = cols.at[occ, pl.ds(pl.multiple_of(virt_place * share, share), share)]
        copy = pltpu.make_async_copy(own.at[occ], mine, local_sem.at[occ, 1])
        copy.start()
        local.append(copy)

    def send_rows(occ):
        for hop, far in enumerate(fars):
            copy = remote(
                own.at[occ], row_slot(occ, aux_place), row_send.at[occ, hop],
                row_recv.at[occ, hop], {"aux": far * 2 + core},
            )
            copy.start()
            row_copies[occ, hop] = copy

    def pass_rows(occ):
        for hop in range(len(fars)):
            row_copies[occ, hop].wait_recv()
            sender = lax.rem(far_place + far_count - 1 - hop, far_count) * 2 + core
            copy = remote(
                row_slot(occ, sender), row_slot(occ, sender), pass_send.at[occ, hop + 1],
                pass_recv.at[occ, hop + 1], sibling,
            )
            copy.start()
            pass_copies[occ, hop + 1] = copy

    waves = [order[at : at + 2] for at in range(0, occs, 2)]
    beats = virt_count - 2 + len(waves)
    for beat in range(beats):
        for at, wave in enumerate(waves):
            step = beat - at
            for occ in wave:
                if step == 0:
                    finish_sum(occ)
                elif 0 < step < virt_count - 1:
                    ring[occ, step - 1].wait_recv()
                    ring[occ, step] = ring_copy(occ, step)
                    ring[occ, step].start()
        if beat == len(waves) - 1:
            for occ in order:
                send_rows(occ)
        if beat == beats - 2:
            for occ in order:
                pass_rows(occ)
    for occ in order:
        ring[occ, virt_count - 2].wait_recv()
    for copy in pass_copies.values():
        copy.wait_recv()
    for copy in local:
        copy.wait()
    for group in (sib_copies, far_copies, ring, row_copies, pass_copies):
        for copy in group.values():
            copy.wait_send()


def gather_fitted(partial_term, aux_count, virt_count):
    occs, virt_local, aux_total = partial_term.shape
    share = virt_local // aux_count
    far_count = aux_count // 2
    dma = pltpu.SemaphoreType.DMA
    return pl.pallas_call(
        functools.partial(gather_kernel, aux_count, virt_count),
        out_shape=(
            jax.ShapeDtypeStruct((occs, virt_local, aux_total), jnp.float32),
            jax.ShapeDtypeStruct((occs, virt_count * share, aux_total), jnp.float32),
        ),
        in_specs=[pl.BlockSpec(memory_space=pltpu.VMEM)],
        out_specs=(pl.BlockSpec(memory_space=pl.ANY), pl.BlockSpec(memory_space=pl.ANY)),
        scratch_shapes=[
            pltpu.VMEM((occs, far_count, share, aux_total), jnp.float32),
            pltpu.VMEM((occs, far_count - 1, share, aux_total), jnp.float32),
            pltpu.VMEM((occs, share, aux_total), jnp.float32),
            dma((occs,)), dma((occs,)),
            dma((occs, far_count - 1)), dma((occs, far_count - 1)),
            dma((occs, far_count - 1)), dma((occs, far_count - 1)),
            dma((occs, far_count)), dma((occs, far_count)),
            dma((occs, virt_count - 1)), dma((occs, virt_count - 1)),
            dma((occs, 2)),
        ],
        compiler_params=pltpu.CompilerParams(
            collective_id=0, has_side_effects=True, vmem_limit_bytes=40 * 1024 * 1024
        ),
        cost_estimate=pl.CostEstimate(flops=0, bytes_accessed=4 * 6 * occs * virt_local * aux_total, transcendentals=0),
    )(partial_term.reshape(occs, far_count, 2, share, aux_total))


def split_parts(values):
    high = values.astype(jnp.bfloat16)
    return high, (values - high.astype(jnp.float32)).astype(jnp.bfloat16)


def density_kernel(
    aux_count, pair, occ_levels, row_levels, col_levels, cols, out,
    w_high, w_low, stage, c_high, c_low, partial, from_sib, from_far,
    stage_sem, sib_send, sib_recv, far_send, far_recv,
):
    occs, virt_local, width = out.shape
    rows = occs * virt_local
    half = rows // 2
    half_occs = occs // 2
    col_count = col_levels.shape[1]
    far_count = aux_count // 2
    aux_place = lax.axis_index("aux")
    core = lax.rem(aux_place, 2)
    far_place = aux_place // 2
    sibling = {"aux": far_place * 2 + 1 - core}

    def fetch(unit, slot):
        target = lax.rem(far_place + 1 + unit // 2, far_count)
        owner = target * 2 + jnp.where(lax.rem(unit, 2) == 0, 1 - core, core)
        return pltpu.make_async_copy(
            cols.at[:, pl.ds(pl.multiple_of(owner * width, 128), width)],
            stage.at[slot], stage_sem.at[slot],
        )

    def sib_copy(hop, part):
        return pltpu.make_async_remote_copy(
            src_ref=partial.at[2 * hop, part], dst_ref=from_sib.at[hop, part],
            send_sem=sib_send.at[hop, part], recv_sem=sib_recv.at[hop, part],
            device_id=sibling, device_id_type=pl.DeviceIdType.MESH,
        )

    def far_copy(hop, part):
        target = lax.rem(far_place + 1 + hop, far_count)
        return pltpu.make_async_remote_copy(
            src_ref=partial.at[2 * hop + 1, part], dst_ref=from_far.at[hop, part],
            send_sem=far_send.at[hop, part], recv_sem=far_recv.at[hop, part],
            device_id={"aux": target * 2 + core}, device_id_type=pl.DeviceIdType.MESH,
        )

    barrier = pltpu.get_barrier_semaphore()
    partners = [sibling] + [
        {"aux": lax.rem(far_place + hop, far_count) * 2 + core} for hop in range(1, far_count)
    ]
    for partner in partners:
        pl.semaphore_signal(barrier, inc=1, device_id=partner, device_id_type=pl.DeviceIdType.MESH)
    fetch(0, 0).start()

    for i in range(occs):
        for j in range(occs):
            direct = pair[pl.ds(i * virt_local, virt_local), pl.ds(j * col_count, col_count)]
            crossed = pair[pl.ds(j * virt_local, virt_local), pl.ds(i * col_count, col_count)]
            denominator = occ_levels[i] + occ_levels[j] - row_levels[...] - col_levels[...]
            high, low = split_parts((2.0 * direct - crossed) / denominator)
            w_high[pl.ds(i * virt_local, virt_local), pl.ds(j * col_count, col_count)] = high
            w_low[pl.ds(i * virt_local, virt_local), pl.ds(j * col_count, col_count)] = low
    pl.semaphore_wait(barrier, len(partners))

    depth = w_high.shape[1]
    units = 2 * far_count
    pieces = occs
    piece = depth // pieces
    for unit in range(units):
        slot = unit % 2
        hop = unit // 2
        if unit + 1 < units:
            fetch(unit + 1, 1 - slot).start()
        fetch(unit, slot).wait()

        @pl.loop(0, pieces)
        def _(step):
            where = pl.ds(pl.multiple_of(step * piece, piece), piece)
            high, low = split_parts(stage[slot, where, :])
            c_high[where, :] = high
            c_low[where, :] = low

        @pl.loop(0, 2)
        def _(part):
            where = pl.ds(pl.multiple_of(part * half, half), half)
            left_high = w_high[where, :]
            right_high = c_high[...]
            total = jnp.dot(left_high, c_low[...], preferred_element_type=jnp.float32)
            total += jnp.dot(w_low[where, :], right_high, preferred_element_type=jnp.float32)
            total += jnp.dot(left_high, right_high, preferred_element_type=jnp.float32)
            if unit % 2 == 0:
                partial[unit, part] = total
                sib_copy(hop, part).start()
            elif hop < far_count - 1:
                sib_copy(hop, part).wait_recv()
                partial[unit, part] = total + from_sib[hop, part]
                far_copy(hop, part).start()
            else:
                sib_copy(hop, part).wait_recv()
                partial[unit, part] = total + from_sib[hop, part]

    for part in range(2):
        total = partial[units - 1, part]
        for hop in range(far_count - 1):
            far_copy(hop, part).wait_recv()
            total = total + from_far[hop, part]
        out[pl.ds(part * half_occs, half_occs)] = total.reshape(half_occs, virt_local, width)
    for part in range(2):
        for hop in range(far_count):
            sib_copy(hop, part).wait_send()
        for hop in range(far_count - 1):
            far_copy(hop, part).wait_send()


def scattered_density(pair, occ_levels, row_levels, col_levels, cols, aux_count):
    occs = occ_levels.shape[0]
    virt_local = row_levels.shape[0]
    rows, depth = pair.shape
    width = cols.shape[1] // aux_count
    far_count = aux_count // 2
    dma = pltpu.SemaphoreType.DMA
    vmem = pl.BlockSpec(memory_space=pltpu.VMEM)
    return pl.pallas_call(
        functools.partial(density_kernel, aux_count),
        out_shape=jax.ShapeDtypeStruct((occs, virt_local, width), jnp.float32),
        in_specs=[
            vmem, pl.BlockSpec(memory_space=pltpu.SMEM), vmem, vmem,
            pl.BlockSpec(memory_space=pl.ANY),
        ],
        out_specs=vmem,
        scratch_shapes=[
            pltpu.VMEM((rows, depth), jnp.bfloat16),
            pltpu.VMEM((rows, depth), jnp.bfloat16),
            pltpu.VMEM((2, depth, width), jnp.float32),
            pltpu.VMEM((depth, width), jnp.bfloat16),
            pltpu.VMEM((depth, width), jnp.bfloat16),
            pltpu.VMEM((2 * far_count, 2, rows // 2, width), jnp.float32),
            pltpu.VMEM((far_count, 2, rows // 2, width), jnp.float32),
            pltpu.VMEM((far_count - 1, 2, rows // 2, width), jnp.float32),
            dma((2,)),
            dma((far_count, 2)), dma((far_count, 2)),
            dma((far_count - 1, 2)), dma((far_count - 1, 2)),
        ],
        compiler_params=pltpu.CompilerParams(
            collective_id=1, has_side_effects=True, vmem_limit_bytes=50 * 1024 * 1024
        ),
        cost_estimate=pl.CostEstimate(
            flops=6 * rows * depth * cols.shape[1], bytes_accessed=4 * depth * cols.shape[1],
            transcendentals=0,
        ),
    )(pair, occ_levels, row_levels[:, None], col_levels[None, :], cols)


def shards(integrals, metric_root, occ_energy, virt_energy, batch_index, virt_order):
    virt_local, batch_count, aux_local = integrals.shape
    aux_total = metric_root.shape[0]
    aux_count = lax.axis_size("aux")
    virt_count = lax.axis_size("virt")
    aux_place = lax.axis_index("aux")
    virt_place = lax.axis_index("virt")
    share = virt_local // aux_count
    occ_levels = select_levels(occ_energy, batch_index)
    virt_levels = select_levels(virt_energy, virt_order)
    row_levels = lax.dynamic_slice_in_dim(virt_levels, virt_place * virt_local, virt_local, 0)
    col_levels = lax.dynamic_slice_in_dim(
        virt_levels.reshape(virt_count, aux_count, share), aux_place, 1, 1
    ).reshape(virt_count * share)

    by_occ = integrals.transpose(1, 0, 2).reshape(batch_count * virt_local, aux_local)
    partial_term = lax.dot_general(
        by_occ,
        metric_root,
        (((1,), (1,)), ((), ())),
        precision=precise,
        preferred_element_type=jnp.float32,
    ).reshape(batch_count, virt_local, aux_total)
    rows, cols = gather_fitted(partial_term, aux_count, virt_count)
    col_count = virt_count * share
    rows2 = rows.reshape(batch_count * virt_local, aux_total)
    cols2 = cols.reshape(batch_count * col_count, aux_total)
    pair = lax.dot_general(
        rows2,
        cols2,
        (((1,), (1,)), ((), ())),
        precision=precise,
        preferred_element_type=jnp.float32,
    )
    if aux_local % 128 == 0 and batch_count % 2 == 0:
        result = scattered_density(pair, occ_levels, row_levels, col_levels, cols2, aux_count)
        return result.transpose(1, 0, 2)
    pair = pair.reshape(batch_count, virt_local, batch_count, col_count)
    swapped = pair.transpose(2, 1, 0, 3)
    denominator = (
        occ_levels[:, None, None, None]
        + occ_levels[None, None, :, None]
        - row_levels[None, :, None, None]
        - col_levels[None, None, None, :]
    )
    weighted = ((2.0 * pair - swapped) / denominator).reshape(
        batch_count * virt_local, batch_count * col_count
    )
    density = jnp.dot(weighted, cols2, precision=precise, preferred_element_type=jnp.float32)
    result = lax.psum_scatter(density, "aux", scatter_dimension=1, tiled=True)
    return result.reshape(batch_count, virt_local, aux_local).transpose(1, 0, 2)


def solution(mesh):
    return jax.shard_map(
        shards,
        mesh=mesh,
        in_specs=(P("virt", None, "aux"), P(None, "aux"), P(), P(), P(), P()),
        out_specs=P("virt", None, "aux"),
        check_vma=False,
    )
```
